256 devices in a mesh: freq: 4 (over z_lo), plane: 64 (over y, z_hi, x, core).
Axes of the slice: x: 4, y: 4, z: 8 (z_hi: 2, z_lo: 4; z = z_hi * 4 + z_lo), core: 2. Of those that a mesh axis runs over, the one named last changes fastest.
Arguments:
- wavefield: float32 [4, 2, 2048, 2048], P('freq', None, 'plane'), may hold values from -6 to 6
- inv_table: float32 [4, 8, 2, 128, 128], P('freq'), may hold values from -1 to 1, as said below
- couple_table: float32 [4, 2, 128, 128], P('freq'), may hold values from -1 to 1
- rhs_table: float32 [4, 8, 2], P('freq'), may hold values from -0.25 to 0.25
- recv_index: int32 [2, 16], replicated, may hold values from 0 to 7
- shot_index: int32 [2, 16], replicated, may hold values from 0 to 7
Outputs:
- migrated: float32 [4, 2, 2048, 2048], P('freq', None, 'plane')
- image: float32 [2, 2048], P(None, 'plane')
The draws below stay inside these ranges and needn't reach their ends.
Inputs may be any that keep to these rules, and one draw needn't show every extreme that they name: `inv_table`: real and imaginary parts of the group inverses.
All inputs are finite; a program needn't handle non-finite values.
Results may differ from the reference program's by a relative error of at most 0.0003.
Values sent between devices are 32-bit elements; how exact they have to be, the bound alone decides.
A program may use at most 64 MiB of HBM per device.

```python
import math
import jax
import jax.numpy as jnp
from jax import lax

NX = 2048
GROUP = 128
NV = 8
DEPTHS = 2
FREQS = 4


def draw_inv_table(key, part):
    noise = jax.random.normal(key, (FREQS, NV, 2, GROUP, GROUP), jnp.float32) * (0.3 / math.sqrt(GROUP))
    unit = jnp.eye(GROUP, dtype=jnp.float32)
    centre = jnp.stack([0.6 * unit, 0.3 * unit])
    return noise + centre[None, None]


def draw_couple_table(key, part):
    centre_value = 0.7
    radius = 0.2
    noise = jax.random.normal(jax.random.fold_in(key, 17), (FREQS, 2, GROUP, GROUP), jnp.float32)
    noise = jnp.clip(noise, -5.0, 5.0) * (radius / math.sqrt(2.0 * GROUP))
    unit = jnp.eye(GROUP, dtype=jnp.float32)
    centre = jnp.stack([centre_value * unit, jnp.zeros_like(unit)])
    return noise + centre[None]


def set_ends(values, stream_key, smallest, largest):
    longest = values.shape.index(max(values.shape))
    spots = []
    for shift in (0, 1):
        where = [jax.random.randint(jax.random.fold_in(stream_key, axis), (), 0, length) for axis, length in enumerate(values.shape)]
        where[longest] = (where[longest] + shift) % values.shape[longest]
        spots.append(tuple(where))
    return values.at[spots[0]].set(smallest).at[spots[1]].set(largest)


def level_of(own_key, dims, pieces, smallest, high):
    level = 1.0
    for dim, shards_of in pieces:
        draws = jax.random.uniform(jax.random.fold_in(jax.random.fold_in(own_key, 6), dim), (shards_of,), jnp.float32, smallest / len(pieces), high / len(pieces))
        level = level * jnp.repeat(jnp.exp(draws), dims[dim] // shards_of).reshape((-1,) + (1,) * (len(dims) - 1 - dim))
    return level


def centred(rng, shape, deviation, limit, cuts=(), kind=jnp.bfloat16):
    drawn = deviation * jax.random.normal(rng, shape, jnp.float32)
    if cuts:
        drawn = drawn * level_of(rng, shape, cuts, -0.22, 0.18)
    return jnp.clip(drawn, -limit, limit).astype(kind)


def setup_inputs(seed: int = 0) -> dict:
    keys = jax.random.split(jax.random.key(seed), 7)
    return {
        "wavefield": centred(keys[0], (FREQS, 2, NX, NX), 1.0, 6.0, ((0, 4), (2, 64)), jnp.float32),
        "inv_table": draw_inv_table(jax.random.fold_in(keys[6], 71), 0),
        "couple_table": draw_couple_table(jax.random.fold_in(keys[6], 71), 0),
        "rhs_table": jnp.clip(jax.random.uniform(keys[3], (FREQS, NV, 2), jnp.float32, -0.25, 0.25) * level_of(keys[3], (FREQS, NV, 2), ((0, 4),), -0.4, 0.0), -0.25, 0.25),
        "recv_index": set_ends(jax.random.randint(keys[4], (DEPTHS, NX // GROUP), 0, NV), jax.random.fold_in(keys[4], 1), 0, NV - 1).astype(jnp.int32),
        "shot_index": set_ends(jax.random.randint(keys[5], (DEPTHS, NX // GROUP), 0, NV), jax.random.fold_in(keys[5], 1), 0, NV - 1).astype(jnp.int32),
    }


highest = lax.Precision.HIGHEST


def complex_product(form, mat_re, mat_im, vec_re, vec_im):
    real_part = jnp.einsum(form, mat_re, vec_re, precision=highest) - jnp.einsum(form, mat_im, vec_im, precision=highest)
    imag_part = jnp.einsum(form, mat_re, vec_im, precision=highest) + jnp.einsum(form, mat_im, vec_re, precision=highest)
    return real_part, imag_part


def line_pass(wave_field, index, inv_table, couple_table, rhs_table):
    freqs = wave_field.shape[0]
    lines = wave_field.shape[2]
    length = wave_field.shape[3]
    group_count = length // GROUP
    levels = jnp.arange(NV, dtype=jnp.int32)
    one_hot = (index[:, None] == levels[None, :]).astype(jnp.float32)
    inv_sel = jnp.einsum('kv,fvcab->fkcab', one_hot, inv_table, precision=highest)
    rhs_sel = jnp.einsum('kv,fvc->fkc', one_hot, rhs_table, precision=highest)
    padded = jnp.pad(wave_field, ((0, 0), (0, 0), (0, 0), (1, 1)))
    second = padded[..., :-2] + padded[..., 2:] - 2.0 * wave_field
    shape = (freqs, lines, group_count, GROUP)
    coef_re = rhs_sel[:, None, :, 0, None]
    coef_im = rhs_sel[:, None, :, 1, None]
    base_re = wave_field[:, 0].reshape(shape)
    base_im = wave_field[:, 1].reshape(shape)
    second_re = second[:, 0].reshape(shape)
    second_im = second[:, 1].reshape(shape)
    source_re = base_re + coef_re * second_re - coef_im * second_im
    source_im = base_im + coef_re * second_im + coef_im * second_re
    local_re, local_im = complex_product('fkab,flkb->flka', inv_sel[:, :, 0], inv_sel[:, :, 1], source_re, source_im)
    couple_re = couple_table[:, 0]
    couple_im = couple_table[:, 1]

    def advance(carry, local):
        add_re, add_im = complex_product('fab,flb->fla', couple_re, couple_im, carry[0], carry[1])
        new_value = (local[0] + add_re, local[1] + add_im)
        return new_value, new_value

    zeros = jnp.zeros((freqs, lines, GROUP), jnp.float32)
    seq_re = jnp.moveaxis(local_re, 2, 0)
    seq_im = jnp.moveaxis(local_im, 2, 0)
    _, (out_re, out_im) = lax.scan(advance, (zeros, zeros), (seq_re, seq_im), reverse=True)
    out_re = jnp.moveaxis(out_re, 0, 2).reshape(freqs, lines, length)
    out_im = jnp.moveaxis(out_im, 0, 2).reshape(freqs, lines, length)
    return jnp.stack([out_re, out_im], axis=1)


def one_frequency(inputs):
    wave_field, inv_table, couple_table, rhs_table, recv_index, shot_index = inputs
    wave_field = wave_field[None]
    inv_table = inv_table[None]
    couple_table = couple_table[None]
    rhs_table = rhs_table[None]
    images = []
    for step_index in range(DEPTHS):
        wave_field = line_pass(wave_field, recv_index[step_index], inv_table, couple_table, rhs_table)
        turned = jnp.swapaxes(wave_field, 2, 3)
        turned = line_pass(turned, shot_index[step_index], inv_table, couple_table, rhs_table)
        wave_field = jnp.swapaxes(turned, 2, 3)
        images.append(jnp.diagonal(wave_field[0, 0]))
    return wave_field[0], jnp.stack(images)


def reference(wavefield, inv_table, couple_table, rhs_table, recv_index, shot_index):
    freqs = wavefield.shape[0]
    recv_all = jnp.broadcast_to(recv_index[None], (freqs,) + recv_index.shape)
    shot_all = jnp.broadcast_to(shot_index[None], (freqs,) + shot_index.shape)
    migrated, images = lax.map(one_frequency, (wavefield, inv_table, couple_table, rhs_table, recv_all, shot_all))
    return migrated, jnp.sum(images, axis=0)
```

```python
import functools

import jax
import jax.numpy as jnp
from jax import lax
from jax.experimental import pallas as pl
from jax.experimental.pallas import tpu as pltpu
from jax.sharding import PartitionSpec as P

NX = 2048
GROUP = 128
DEPTHS = 2
NV = 8
GROUPS = NX // GROUP
PLANE = 64
FREQ = 4
LINES = NX // PLANE
HALF = LINES // 2
UNROLL = 4
MESH = pl.DeviceIdType.MESH
F32 = jnp.float32
BF16 = jnp.bfloat16


def split(values):
    high = values.astype(BF16)
    low = (values - high.astype(F32)).astype(BF16)
    return high, low


def dot_nt(left, right):
    return lax.dot_general(left, right, (((1,), (1,)), ((), ())), preferred_element_type=F32)


def dot_nn(left, right):
    return lax.dot_general(left, right, (((1,), (0,)), ((), ())), preferred_element_type=F32)


def product(dot, values, mat_high, mat_low):
    count = values.shape[0]
    high, low = split(values)
    both = dot(jnp.concatenate([high, low], axis=0), mat_high)
    return both[:count] + both[count:] + dot(high, mat_low)


def store_complex(high_ref, low_ref, at, real, imag):
    re_high, re_low = split(real)
    im_high, im_low = split(imag)
    for ref, re_part, im_part in ((high_ref, re_high, im_high), (low_ref, re_low, im_low)):
        ref[at, :GROUP, :GROUP] = re_part
        ref[at, :GROUP, GROUP:] = -im_part
        ref[at, GROUP:, :GROUP] = im_part
        ref[at, GROUP:, GROUP:] = re_part


def swap_blocks(tiles):
    shape = tiles[0].shape
    axis = len(shape) - 1
    lane = lax.broadcasted_iota(jnp.int32, shape, axis)
    lower = lane < 64
    even = (lane // 32) % 2 == 0
    first = [None] * 4
    for a in (0, 1):
        first[a] = jnp.where(lower, tiles[a], pltpu.roll(tiles[a + 2], 64, axis))
        first[a + 2] = jnp.where(lower, pltpu.roll(tiles[a], 64, axis), tiles[a + 2])
    out = [None] * 4
    for a in (0, 2):
        out[a] = jnp.where(even, first[a], pltpu.roll(first[a + 1], 32, axis))
        out[a + 1] = jnp.where(even, pltpu.roll(first[a], 96, axis), first[a + 1])
    return out


def line_pass(src, dst, lines, index, step, inv_high, inv_low, pow_high, pow_low, rhs):
    lane = lax.broadcasted_iota(jnp.int32, (lines, GROUP), 1)
    first = lane == 0
    last = lane == GROUP - 1

    def second_difference(k, part):
        cols = slice(part * GROUP, (part + 1) * GROUP)
        here = src[k + 1, :, cols]
        left = pltpu.roll(jnp.where(last, src[k, :, cols], here), 1, 1)
        right = pltpu.roll(jnp.where(first, src[k + 2, :, cols], here), GROUP - 1, 1)
        return here, left + right - 2.0 * here

    @pl.loop(0, GROUPS // UNROLL)
    def _(outer):
        for inner in range(UNROLL):
            k = outer * UNROLL + inner
            level = index[step, k]
            coef_re = rhs[0, level, 0]
            coef_im = rhs[0, level, 1]
            base_re, second_re = second_difference(k, 0)
            base_im, second_im = second_difference(k, 1)
            source_re = base_re + coef_re * second_re - coef_im * second_im
            source_im = base_im + coef_re * second_im + coef_im * second_re
            source = jnp.concatenate([source_re, source_im], axis=1)
            dst[k + 1] = product(dot_nt, source, inv_high[level], inv_low[level])

    for at, reach in enumerate((1, 2, 4, 8)):
        count = GROUPS - reach
        moved = dst[1 + reach : 1 + GROUPS].reshape(count * lines, 2 * GROUP)
        added = product(dot_nt, moved, pow_high[at], pow_low[at])
        dst[1 : 1 + count] = dst[1 : 1 + count] + added.reshape(count, lines, 2 * GROUP)


def kernel(
    wave_hbm, inv_hbm, couple_hbm, rhs, recv_index, shot_index,
    out, image,
    wave, inv, couple, inv_high, inv_low, pow_high, pow_low,
    field_a, field_b, unit, column_a, column_b,
    fsend, frecv, bsend, brecv,
    vsend, vrecv, wsend, wrecv, isend, irecv,
    in_sem, fwd_send, fwd_recv, back_send, back_recv, img_send, img_recv,
):
    me = lax.axis_index("plane")
    fr = lax.axis_index("freq")
    cross = me % 8
    along = me // 8

    copies = [
        pltpu.make_async_copy(couple_hbm.at[0], couple, in_sem.at[0]),
        pltpu.make_async_copy(inv_hbm.at[0], inv, in_sem.at[1]),
        pltpu.make_async_copy(wave_hbm.at[0], wave, in_sem.at[2]),
    ]
    for copy in copies:
        copy.start()

    def partner(step):
        return (me + step * 9) % PLANE

    barrier = pltpu.get_barrier_semaphore()

    @pl.loop(1, PLANE)
    def _(step):
        pl.semaphore_signal(barrier, inc=1, device_id=(fr, partner(step)), device_id_type=MESH)

    @pl.loop(1, FREQ)
    def _(step):
        pl.semaphore_signal(barrier, inc=1, device_id=((fr + step) % FREQ, me), device_id_type=MESH)

    passes = dict(inv_high=inv_high, inv_low=inv_low, pow_high=pow_high, pow_low=pow_low, rhs=rhs)

    for ref in (field_a, field_b, unit, column_a, column_b):
        pad = jnp.zeros(ref.shape[1:], F32)
        ref[0] = pad
        ref[GROUPS + 1] = pad

    copies[0].wait()
    power_re = couple[0]
    power_im = couple[1]
    for at in range(4):
        store_complex(pow_high, pow_low, at, power_re, power_im)
        if at < 3:
            column = jnp.concatenate([power_re, power_im], axis=0)
            col_high, col_low = split(column)
            high = pow_high[at]
            low = pow_low[at]
            square = dot_nn(high, col_high) + dot_nn(low, col_high) + dot_nn(high, col_low)
            power_re = square[:GROUP]
            power_im = square[GROUP:]
    copies[1].wait()

    @pl.loop(0, NV)
    def _(level):
        store_complex(inv_high, inv_low, level, inv[level, 0], inv[level, 1])

    copies[2].wait()
    for k in range(GROUPS):
        for part in range(2):
            field_a[k + 1, :, part * GROUP : (part + 1) * GROUP] = wave[part, :, k * GROUP : (k + 1) * GROUP]

    line_pass(field_a, field_b, LINES, recv_index, 0, **passes)
    line_pass(field_b, field_a, LINES, recv_index, 1, **passes)

    for big in range(4):
        turned = [
            field_a[1 + 4 * big : 5 + 4 * big, :, part * GROUP : (part + 1) * GROUP]
            .reshape(GROUP, GROUP).T.reshape(4, 4, 8, GROUP)
            for part in range(2)
        ]
        for h in range(2):
            tiles = [turned[part][:, 2 * h + b] for part in range(2) for b in range(2)]
            for y, tile in enumerate(swap_blocks(tiles)):
                first = 4 * (4 * big + y)
                fsend[h, first : first + 4] = tile

    pl.semaphore_wait(barrier, PLANE - 1 + FREQ - 1)

    def exchange(src, dst, h, send, recv):
        @pl.loop(1, PLANE)
        def _(step):
            to = partner(step)
            pltpu.make_async_remote_copy(
                src_ref=src.at[h, to],
                dst_ref=dst.at[h, me],
                send_sem=send.at[h],
                recv_sem=recv.at[h],
                device_id=(fr, to),
                device_id_type=MESH,
            ).start()

        dst[h, me] = src[h, me]

    def all_bytes(ref, h, sem):
        pltpu.make_async_copy(ref.at[h, pl.ds(0, PLANE - 1)], ref.at[h, pl.ds(0, PLANE - 1)], sem.at[h]).wait()

    for h in range(2):
        exchange(fsend, frecv, h, fwd_send, fwd_recv)

    spot = lax.broadcasted_iota(jnp.int32, (LINES, GROUP), 1) - lax.broadcasted_iota(
        jnp.int32, (LINES, GROUP), 0
    )
    for k in range(GROUPS):
        unit[k + 1, :, :GROUP] = (spot == LINES * me - k * GROUP).astype(F32)
        unit[k + 1, :, GROUP:] = jnp.zeros((LINES, GROUP), F32)
    line_pass(unit, field_a, LINES, shot_index, 0, **passes)
    for k in range(GROUPS):
        both = field_a[k + 1] * field_b[k + 1]
        terms = both[:, :GROUP] - both[:, GROUP:]
        vsend[k % 2, k // 2 : k // 2 + 1] = jnp.sum(terms, axis=0, keepdims=True)

    @pl.loop(1, 8)
    def _(step):
        to = (cross + step) % 8
        pltpu.make_async_remote_copy(
            src_ref=vsend.at[to // 4],
            dst_ref=vrecv.at[cross],
            send_sem=img_send.at[0],
            recv_sem=img_recv.at[0],
            device_id=(fr, along * 8 + to),
            device_id_type=MESH,
        ).start()

    vrecv[cross] = vsend[cross // 4]

    lane_row = lax.broadcasted_iota(jnp.int32, (1, GROUP), 1)
    mine = lane_row // LINES == me % 4
    diagonal = jnp.zeros((1, GROUP), F32)
    for h in range(2):
        all_bytes(frecv, h, fwd_recv)
        arrived = frecv[h].reshape(GROUPS, 4, 8, GROUP)
        tiles = swap_blocks([arrived[:, q] for q in range(4)])
        for part in range(2):
            for b in range(2):
                column_a[1 : 1 + GROUPS, b * 8 : b * 8 + 8, part * GROUP : (part + 1) * GROUP] = tiles[2 * part + b]
        line_pass(column_a, column_b, HALF, shot_index, 0, **passes)
        line_pass(column_b, column_a, HALF, shot_index, 1, **passes)
        tiles = [
            column_a[1 : 1 + GROUPS, b * 8 : b * 8 + 8, part * GROUP : (part + 1) * GROUP]
            for part in range(2)
            for b in range(2)
        ]
        bsend[h] = jnp.stack(swap_blocks(tiles), axis=1).reshape(PLANE, 8, GROUP)
        exchange(bsend, brecv, h, back_send, back_recv)
        block = column_a[me // 4 + 1, :, :GROUP]
        row = lax.broadcasted_iota(jnp.int32, (HALF, GROUP), 0)
        lane = lax.broadcasted_iota(jnp.int32, (HALF, GROUP), 1)
        kept = jnp.where(lane == (me % 4) * LINES + h * HALF + row, block, 0.0)
        diagonal = diagonal + jnp.sum(kept, axis=0, keepdims=True)
        if h == 0:
            pltpu.make_async_copy(vrecv.at[pl.ds(0, 7)], vrecv.at[pl.ds(0, 7)], img_recv.at[0]).wait()
            sums = jnp.sum(vrecv[...], axis=0)
            for j in range(8):
                wsend[j] = sums[j : j + 1]

            @pl.loop(1, 8)
            def _(step):
                to = (along + step) % 8
                pltpu.make_async_remote_copy(
                    src_ref=wsend.at[to],
                    dst_ref=wrecv.at[along],
                    send_sem=img_send.at[1],
                    recv_sem=img_recv.at[1],
                    device_id=(fr, to * 8 + cross),
                    device_id_type=MESH,
                ).start()

            wrecv[along] = wsend[along]

    pltpu.make_async_copy(wrecv.at[pl.ds(0, 7)], wrecv.at[pl.ds(0, 7)], img_recv.at[1]).wait()
    summed = jnp.where(mine, jnp.sum(wrecv[...], axis=0), 0.0)

    def folded(values):
        values = values + pltpu.roll(values, 64, 1)
        return values + pltpu.roll(values, 32, 1)

    isend[...] = jnp.zeros((8, GROUP), F32)
    isend[0:1] = folded(summed)
    isend[1:2] = folded(diagonal)

    @pl.loop(1, FREQ)
    def _(step):
        pltpu.make_async_remote_copy(
            src_ref=isend,
            dst_ref=irecv.at[fr],
            send_sem=img_send.at[2],
            recv_sem=img_recv.at[2],
            device_id=((fr + step) % FREQ, me),
            device_id_type=MESH,
        ).start()

    irecv[fr] = isend[...]

    for h in range(2):
        all_bytes(brecv, h, back_recv)
    for big in range(4):
        turned = [[None] * 4, [None] * 4]
        for h in range(2):
            tiles = swap_blocks([brecv[h, 4 * (4 * big + y) : 4 * (4 * big + y) + 4] for y in range(4)])
            for part in range(2):
                for b in range(2):
                    turned[part][2 * h + b] = tiles[2 * part + b]
        for part in range(2):
            block = jnp.stack(turned[part], axis=1).reshape(GROUP, GROUP).T
            for y in range(4):
                at = (4 * big + y) * GROUP
                out[0, part, :, at : at + GROUP] = block[y * LINES : (y + 1) * LINES]

    pltpu.make_async_copy(irecv.at[pl.ds(0, 3)], irecv.at[pl.ds(0, 3)], img_recv.at[2]).wait()
    image[...] = (irecv[0] + irecv[1] + irecv[2] + irecv[3])[:2, :LINES]

    for h in range(2):
        all_bytes(fsend, h, fwd_send)
        all_bytes(bsend, h, back_send)
    pltpu.make_async_copy(vrecv.at[pl.ds(0, 7)], vrecv.at[pl.ds(0, 7)], img_send.at[0]).wait()
    pltpu.make_async_copy(wrecv.at[pl.ds(0, 7)], wrecv.at[pl.ds(0, 7)], img_send.at[1]).wait()
    pltpu.make_async_copy(irecv.at[pl.ds(0, 3)], irecv.at[pl.ds(0, 3)], img_send.at[2]).wait()


def shards(wavefield, inv_table, couple_table, rhs_table, recv_index, shot_index):
    hbm = pl.BlockSpec(memory_space=pl.ANY)
    vmem = pl.BlockSpec(memory_space=pltpu.VMEM)
    smem = pl.BlockSpec(memory_space=pltpu.SMEM)
    tiles = (2, PLANE, 8, GROUP)
    wide = 2 * GROUP
    return pl.pallas_call(
        kernel,
        out_shape=(
            jax.ShapeDtypeStruct((1, 2, LINES, NX), F32),
            jax.ShapeDtypeStruct((DEPTHS, LINES), F32),
        ),
        in_specs=[hbm, hbm, hbm, smem, smem, smem],
        out_specs=(vmem, vmem),
        scratch_shapes=[
            pltpu.VMEM((2, LINES, NX), F32),
            pltpu.VMEM((NV, 2, GROUP, GROUP), F32),
            pltpu.VMEM((2, GROUP, GROUP), F32),
            pltpu.VMEM((NV, wide, wide), BF16),
            pltpu.VMEM((NV, wide, wide), BF16),
            pltpu.VMEM((4, wide, wide), BF16),
            pltpu.VMEM((4, wide, wide), BF16),
            pltpu.VMEM((GROUPS + 2, LINES, wide), F32),
            pltpu.VMEM((GROUPS + 2, LINES, wide), F32),
            pltpu.VMEM((GROUPS + 2, LINES, wide), F32),
            pltpu.VMEM((GROUPS + 2, HALF, wide), F32),
            pltpu.VMEM((GROUPS + 2, HALF, wide), F32),
            pltpu.VMEM(tiles, F32),
            pltpu.VMEM(tiles, F32),
            pltpu.VMEM(tiles, F32),
            pltpu.VMEM(tiles, F32),
            pltpu.VMEM((2, 8, GROUP), F32),
            pltpu.VMEM((8, 8, GROUP), F32),
            pltpu.VMEM((8, 1, GROUP), F32),
            pltpu.VMEM((8, 1, GROUP), F32),
            pltpu.VMEM((8, GROUP), F32),
            pltpu.VMEM((FREQ, 8, GROUP), F32),
            pltpu.SemaphoreType.DMA((3,)),
            pltpu.SemaphoreType.DMA((2,)),
            pltpu.SemaphoreType.DMA((2,)),
            pltpu.SemaphoreType.DMA((2,)),
            pltpu.SemaphoreType.DMA((2,)),
            pltpu.SemaphoreType.DMA((3,)),
            pltpu.SemaphoreType.DMA((3,)),
        ],
        compiler_params=pltpu.CompilerParams(
            collective_id=0, has_side_effects=True, vmem_limit_bytes=40 << 20
        ),
        cost_estimate=pl.CostEstimate(
            flops=5_000_000_000, bytes_accessed=3_000_000, transcendentals=0
        ),
    )(wavefield, inv_table, couple_table, rhs_table, recv_index, shot_index)


def solution(mesh):
    placed = (
        P("freq", None, "plane", None),
        P("freq", None, None, None, None),
        P("freq", None, None, None),
        P("freq", None, None),
        P(),
        P(),
    )
    return jax.shard_map(
        shards,
        mesh=mesh,
        in_specs=placed,
        out_specs=(P("freq", None, "plane", None), P(None, "plane")),
        check_vma=False,
    )
```

```python
import functools

import jax
import jax.numpy as jnp
from jax import lax
from jax.experimental import pallas as pl
from jax.experimental.pallas import tpu as pltpu
from jax.sharding import PartitionSpec as P

NX = 2048
GROUP = 128
DEPTHS = 2
NV = 8
GROUPS = NX // GROUP
PLANE = 64
FREQ = 4
LINES = NX // PLANE
HALF = LINES // 2
MESH = pl.DeviceIdType.MESH
F32 = jnp.float32
BF16 = jnp.bfloat16


def split(values):
    high = values.astype(BF16)
    low = (values - high.astype(F32)).astype(BF16)
    return high, low


def dot(left, right):
    return lax.dot_general(left, right, (((1,), (0,)), ((), ())), preferred_element_type=F32)


def product(values, mat_high, mat_low):
    count = values.shape[0]
    high, low = split(values)
    both = dot(jnp.concatenate([high, low], axis=0), mat_high)
    return both[:count] + both[count:] + dot(high, mat_low)


def store_complex(high_ref, low_ref, at, real, imag):
    re_high, re_low = split(real)
    im_high, im_low = split(imag)
    for ref, re_part, im_part in ((high_ref, re_high, im_high), (low_ref, re_low, im_low)):
        ref[at, :GROUP, :GROUP] = re_part
        ref[at, :GROUP, GROUP:] = im_part
        ref[at, GROUP:, :GROUP] = -im_part
        ref[at, GROUP:, GROUP:] = re_part


def swap_blocks(tiles):
    shape = tiles[0].shape
    axis = len(shape) - 1
    lane = lax.broadcasted_iota(jnp.int32, shape, axis)
    lower = lane < 64
    even = (lane // 32) % 2 == 0
    first = [None] * 4
    for a in (0, 1):
        first[a] = jnp.where(lower, tiles[a], pltpu.roll(tiles[a + 2], 64, axis))
        first[a + 2] = jnp.where(lower, pltpu.roll(tiles[a], 64, axis), tiles[a + 2])
    out = [None] * 4
    for a in (0, 2):
        out[a] = jnp.where(even, first[a], pltpu.roll(first[a + 1], 32, axis))
        out[a + 1] = jnp.where(even, pltpu.roll(first[a], 96, axis), first[a + 1])
    return out


def line_pass(src, dst, lines, index, step, inv_high, inv_low, pow_high, pow_low, rhs):
    lane = lax.broadcasted_iota(jnp.int32, (lines, GROUP), 1)
    first = lane == 0
    last = lane == GROUP - 1

    def second_difference(k, part):
        cols = slice(part * GROUP, (part + 1) * GROUP)
        here = src[k + 1, :, cols]
        left = pltpu.roll(jnp.where(last, src[k, :, cols], here), 1, 1)
        right = pltpu.roll(jnp.where(first, src[k + 2, :, cols], here), GROUP - 1, 1)
        return here, left + right - 2.0 * here

    for k in range(GROUPS):
        level = index[step, k]
        coef_re = rhs[0, 0, level]
        coef_im = rhs[0, 1, level]
        base_re, second_re = second_difference(k, 0)
        base_im, second_im = second_difference(k, 1)
        source_re = base_re + coef_re * second_re - coef_im * second_im
        source_im = base_im + coef_re * second_im + coef_im * second_re
        source = jnp.concatenate([source_re, source_im], axis=1)
        dst[k + 1] = product(source, inv_high[level], inv_low[level])

    for at, reach in enumerate((1, 2, 4, 8)):
        count = GROUPS - reach
        moved = dst[1 + reach : 1 + GROUPS].reshape(count * lines, 2 * GROUP)
        added = product(moved, pow_high[at], pow_low[at])
        dst[1 : 1 + count] = dst[1 : 1 + count] + added.reshape(count, lines, 2 * GROUP)


def kernel(
    wave_hbm, inv_hbm, couple_hbm, rhs, recv_index, shot_index,
    out, image,
    wave, inv, couple, inv_high, inv_low, pow_high, pow_low,
    field_a, field_b, unit, column_a, column_b,
    fsend, frecv, bsend, brecv,
    vsend, vrecv, wsend, wrecv, isend, irecv,
    in_sem, fwd_send, fwd_recv, back_send, back_recv, img_send, img_recv,
):
    me = lax.axis_index("plane")
    fr = lax.axis_index("freq")
    cross = me % 8
    along = me // 8

    copies = [
        pltpu.make_async_copy(couple_hbm.at[0], couple, in_sem.at[0]),
        pltpu.make_async_copy(inv_hbm.at[0], inv, in_sem.at[1]),
        pltpu.make_async_copy(wave_hbm.at[0], wave, in_sem.at[2]),
    ]
    for copy in copies:
        copy.start()

    def partner(step):
        return (me + step * 33) % PLANE

    barrier = pltpu.get_barrier_semaphore()

    @pl.loop(1, PLANE)
    def _(step):
        pl.semaphore_signal(barrier, inc=1, device_id=(fr, partner(step)), device_id_type=MESH)

    @pl.loop(1, FREQ)
    def _(step):
        pl.semaphore_signal(barrier, inc=1, device_id=((fr + step) % FREQ, me), device_id_type=MESH)

    passes = dict(inv_high=inv_high, inv_low=inv_low, pow_high=pow_high, pow_low=pow_low, rhs=rhs)

    for ref in (field_a, field_b, unit, column_a, column_b):
        pad = jnp.zeros(ref.shape[1:], F32)
        ref[0] = pad
        ref[GROUPS + 1] = pad

    copies[0].wait()
    power_re = couple[0].T
    power_im = couple[1].T
    for at in range(4):
        store_complex(pow_high, pow_low, at, power_re, power_im)
        if at < 3:
            row = jnp.concatenate([power_re, power_im], axis=1)
            square = product(row, pow_high[at], pow_low[at])
            power_re = square[:, :GROUP]
            power_im = square[:, GROUP:]
    copies[1].wait()

    @pl.loop(0, NV)
    def _(level):
        store_complex(inv_high, inv_low, level, inv[level, 0].T, inv[level, 1].T)

    copies[2].wait()
    for k in range(GROUPS):
        for part in range(2):
            field_a[k + 1, :, part * GROUP : (part + 1) * GROUP] = wave[part, :, k * GROUP : (k + 1) * GROUP]

    line_pass(field_a, field_b, LINES, recv_index, 0, **passes)
    line_pass(field_b, field_a, LINES, recv_index, 1, **passes)

    for big in range(4):
        turned = [
            field_a[1 + 4 * big : 5 + 4 * big, :, part * GROUP : (part + 1) * GROUP]
            .reshape(GROUP, GROUP).T.reshape(4, 4, 8, GROUP)
            for part in range(2)
        ]
        for h in range(2):
            tiles = [turned[part][:, 2 * h + b] for part in range(2) for b in range(2)]
            for y, tile in enumerate(swap_blocks(tiles)):
                first = 4 * (4 * big + y)
                fsend[h, first : first + 4] = tile

    pl.semaphore_wait(barrier, PLANE - 1 + FREQ - 1)

    def exchange(src, dst, h, send, recv):
        @pl.loop(1, PLANE)
        def _(step):
            to = partner(step)
            pltpu.make_async_remote_copy(
                src_ref=src.at[h, to],
                dst_ref=dst.at[h, me],
                send_sem=send.at[h],
                recv_sem=recv.at[h],
                device_id=(fr, to),
                device_id_type=MESH,
            ).start()

        dst[h, me] = src[h, me]

    def all_bytes(ref, h, sem):
        pltpu.make_async_copy(ref.at[h, pl.ds(0, PLANE - 1)], ref.at[h, pl.ds(0, PLANE - 1)], sem.at[h]).wait()

    for h in range(2):
        exchange(fsend, frecv, h, fwd_send, fwd_recv)

    spot = lax.broadcasted_iota(jnp.int32, (LINES, GROUP), 1) - lax.broadcasted_iota(
        jnp.int32, (LINES, GROUP), 0
    )
    for k in range(GROUPS):
        unit[k + 1, :, :GROUP] = (spot == LINES * me - k * GROUP).astype(F32)
        unit[k + 1, :, GROUP:] = jnp.zeros((LINES, GROUP), F32)
    line_pass(unit, field_a, LINES, shot_index, 0, **passes)
    for k in range(GROUPS):
        both = field_a[k + 1] * field_b[k + 1]
        terms = both[:, :GROUP] - both[:, GROUP:]
        vsend[k % 2, k // 2 : k // 2 + 1] = jnp.sum(terms, axis=0, keepdims=True)

    @pl.loop(1, 8)
    def _(step):
        to = (cross + step) % 8
        pltpu.make_async_remote_copy(
            src_ref=vsend.at[to // 4],
            dst_ref=vrecv.at[cross],
            send_sem=img_send.at[0],
            recv_sem=img_recv.at[0],
            device_id=(fr, along * 8 + to),
            device_id_type=MESH,
        ).start()

    vrecv[cross] = vsend[cross // 4]

    lane_row = lax.broadcasted_iota(jnp.int32, (1, GROUP), 1)
    mine = lane_row // LINES == me % 4
    diagonal = jnp.zeros((1, GROUP), F32)
    for h in range(2):
        all_bytes(frecv, h, fwd_recv)
        arrived = frecv[h].reshape(GROUPS, 4, 8, GROUP)
        tiles = swap_blocks([arrived[:, q] for q in range(4)])
        for part in range(2):
            for b in range(2):
                column_a[1 : 1 + GROUPS, b * 8 : b * 8 + 8, part * GROUP : (part + 1) * GROUP] = tiles[2 * part + b]
        line_pass(column_a, column_b, HALF, shot_index, 0, **passes)
        line_pass(column_b, column_a, HALF, shot_index, 1, **passes)
        tiles = [
            column_a[1 : 1 + GROUPS, b * 8 : b * 8 + 8, part * GROUP : (part + 1) * GROUP]
            for part in range(2)
            for b in range(2)
        ]
        bsend[h] = jnp.stack(swap_blocks(tiles), axis=1).reshape(PLANE, 8, GROUP)
        exchange(bsend, brecv, h, back_send, back_recv)
        block = column_a[me // 4 + 1, :, :GROUP]
        row = lax.broadcasted_iota(jnp.int32, (HALF, GROUP), 0)
        lane = lax.broadcasted_iota(jnp.int32, (HALF, GROUP), 1)
        kept = jnp.where(lane == (me % 4) * LINES + h * HALF + row, block, 0.0)
        diagonal = diagonal + jnp.sum(kept, axis=0, keepdims=True)
        if h == 0:
            pltpu.make_async_copy(vrecv.at[pl.ds(0, 7)], vrecv.at[pl.ds(0, 7)], img_recv.at[0]).wait()
            sums = jnp.sum(vrecv[...], axis=0)
            for j in range(8):
                wsend[j] = sums[j : j + 1]

            @pl.loop(1, 8)
            def _(step):
                to = (along + step) % 8
                pltpu.make_async_remote_copy(
                    src_ref=wsend.at[to],
                    dst_ref=wrecv.at[along],
                    send_sem=img_send.at[1],
                    recv_sem=img_recv.at[1],
                    device_id=(fr, to * 8 + cross),
                    device_id_type=MESH,
                ).start()

            wrecv[along] = wsend[along]

    pltpu.make_async_copy(wrecv.at[pl.ds(0, 7)], wrecv.at[pl.ds(0, 7)], img_recv.at[1]).wait()
    summed = jnp.where(mine, jnp.sum(wrecv[...], axis=0), 0.0)

    def folded(values):
        values = values + pltpu.roll(values, 64, 1)
        return values + pltpu.roll(values, 32, 1)

    isend[...] = jnp.zeros((8, GROUP), F32)
    isend[0:1] = folded(summed)
    isend[1:2] = folded(diagonal)

    @pl.loop(1, FREQ)
    def _(step):
        pltpu.make_async_remote_copy(
            src_ref=isend,
            dst_ref=irecv.at[fr],
            send_sem=img_send.at[2],
            recv_sem=img_recv.at[2],
            device_id=((fr + step) % FREQ, me),
            device_id_type=MESH,
        ).start()

    irecv[fr] = isend[...]

    for h in range(2):
        all_bytes(brecv, h, back_recv)
    for big in range(4):
        turned = [[None] * 4, [None] * 4]
        for h in range(2):
            tiles = swap_blocks([brecv[h, 4 * (4 * big + y) : 4 * (4 * big + y) + 4] for y in range(4)])
            for part in range(2):
                for b in range(2):
                    turned[part][2 * h + b] = tiles[2 * part + b]
        for part in range(2):
            block = jnp.stack(turned[part], axis=1).reshape(GROUP, GROUP).T
            for y in range(4):
                at = (4 * big + y) * GROUP
                out[0, part, :, at : at + GROUP] = block[y * LINES : (y + 1) * LINES]

    pltpu.make_async_copy(irecv.at[pl.ds(0, 3)], irecv.at[pl.ds(0, 3)], img_recv.at[2]).wait()
    image[...] = (irecv[0] + irecv[1] + irecv[2] + irecv[3])[:2, :LINES]

    for h in range(2):
        all_bytes(fsend, h, fwd_send)
        all_bytes(bsend, h, back_send)
    pltpu.make_async_copy(vrecv.at[pl.ds(0, 7)], vrecv.at[pl.ds(0, 7)], img_send.at[0]).wait()
    pltpu.make_async_copy(wrecv.at[pl.ds(0, 7)], wrecv.at[pl.ds(0, 7)], img_send.at[1]).wait()
    pltpu.make_async_copy(irecv.at[pl.ds(0, 3)], irecv.at[pl.ds(0, 3)], img_send.at[2]).wait()


def shards(wavefield, inv_table, couple_table, rhs_table, recv_index, shot_index):
    hbm = pl.BlockSpec(memory_space=pltpu.HBM)
    vmem = pl.BlockSpec(memory_space=pltpu.VMEM)
    smem = pl.BlockSpec(memory_space=pltpu.SMEM)
    tiles = (2, PLANE, 8, GROUP)
    wide = 2 * GROUP
    return pl.pallas_call(
        kernel,
        out_shape=(
            jax.ShapeDtypeStruct((1, 2, LINES, NX), F32),
            jax.ShapeDtypeStruct((DEPTHS, LINES), F32),
        ),
        in_specs=[hbm, hbm, hbm, smem, smem, smem],
        out_specs=(vmem, vmem),
        scratch_shapes=[
            pltpu.VMEM((2, LINES, NX), F32),
            pltpu.VMEM((NV, 2, GROUP, GROUP), F32),
            pltpu.VMEM((2, GROUP, GROUP), F32),
            pltpu.VMEM((NV, wide, wide), BF16),
            pltpu.VMEM((NV, wide, wide), BF16),
            pltpu.VMEM((4, wide, wide), BF16),
            pltpu.VMEM((4, wide, wide), BF16),
            pltpu.VMEM((GROUPS + 2, LINES, wide), F32),
            pltpu.VMEM((GROUPS + 2, LINES, wide), F32),
            pltpu.VMEM((GROUPS + 2, LINES, wide), F32),
            pltpu.VMEM((GROUPS + 2, HALF, wide), F32),
            pltpu.VMEM((GROUPS + 2, HALF, wide), F32),
            pltpu.VMEM(tiles, F32),
            pltpu.VMEM(tiles, F32),
            pltpu.VMEM(tiles, F32),
            pltpu.VMEM(tiles, F32),
            pltpu.VMEM((2, 8, GROUP), F32),
            pltpu.VMEM((8, 8, GROUP), F32),
            pltpu.VMEM((8, 1, GROUP), F32),
            pltpu.VMEM((8, 1, GROUP), F32),
            pltpu.VMEM((8, GROUP), F32),
            pltpu.VMEM((FREQ, 8, GROUP), F32),
            pltpu.SemaphoreType.DMA((3,)),
            pltpu.SemaphoreType.DMA((2,)),
            pltpu.SemaphoreType.DMA((2,)),
            pltpu.SemaphoreType.DMA((2,)),
            pltpu.SemaphoreType.DMA((2,)),
            pltpu.SemaphoreType.DMA((3,)),
            pltpu.SemaphoreType.DMA((3,)),
        ],
        compiler_params=pltpu.CompilerParams(
            collective_id=0, has_side_effects=True, vmem_limit_bytes=58 << 20
        ),
        cost_estimate=pl.CostEstimate(
            flops=5_000_000_000, bytes_accessed=3_000_000, transcendentals=0
        ),
    )(wavefield, inv_table, couple_table, jnp.swapaxes(rhs_table, 1, 2), recv_index, shot_index)


def solution(mesh):
    placed = (
        P("freq", None, "plane", None),
        P("freq", None, None, None, None),
        P("freq", None, None, None),
        P("freq", None, None),
        P(),
        P(),
    )
    return jax.shard_map(
        shards,
        mesh=mesh,
        in_specs=placed,
        out_specs=(P("freq", None, "plane", None), P(None, "plane")),
        check_vma=False,
    )
```

```python
import functools

import jax
import jax.numpy as jnp
from jax import lax
from jax.experimental import pallas as pl
from jax.experimental.pallas import tpu as pltpu
from jax.sharding import PartitionSpec as P

NX = 2048
GROUP = 128
DEPTHS = 2
NV = 8
GROUPS = NX // GROUP
PLANE = 64
FREQ = 4
LINES = NX // PLANE
HALF = LINES // 2
MESH = pl.DeviceIdType.MESH
F32 = jnp.float32
BF16 = jnp.bfloat16


def split(values):
    high = values.astype(BF16)
    low = (values - high.astype(F32)).astype(BF16)
    return high, low


def dot(left, right):
    return lax.dot_general(left, right, (((1,), (0,)), ((), ())), preferred_element_type=F32)


def product(values, mat_high, mat_low):
    count = values.shape[0]
    high, low = split(values)
    both = dot(jnp.concatenate([high, low], axis=0), mat_high)
    return both[:count] + both[count:] + dot(high, mat_low)


def store_complex(high_ref, low_ref, at, real, imag):
    re_high, re_low = split(real)
    im_high, im_low = split(imag)
    for ref, re_part, im_part in ((high_ref, re_high, im_high), (low_ref, re_low, im_low)):
        ref[at, :GROUP, :GROUP] = re_part
        ref[at, :GROUP, GROUP:] = im_part
        ref[at, GROUP:, :GROUP] = -im_part
        ref[at, GROUP:, GROUP:] = re_part


def swap_blocks(tiles):
    shape = tiles[0].shape
    axis = len(shape) - 1
    lane = lax.broadcasted_iota(jnp.int32, shape, axis)
    lower = lane < 64
    even = (lane // 32) % 2 == 0
    first = [None] * 4
    for a in (0, 1):
        first[a] = jnp.where(lower, tiles[a], pltpu.roll(tiles[a + 2], 64, axis))
        first[a + 2] = jnp.where(lower, pltpu.roll(tiles[a], 64, axis), tiles[a + 2])
    out = [None] * 4
    for a in (0, 2):
        out[a] = jnp.where(even, first[a], pltpu.roll(first[a + 1], 32, axis))
        out[a + 1] = jnp.where(even, pltpu.roll(first[a], 96, axis), first[a + 1])
    return out


def line_pass(src, dst, lines, index, step, inv_high, inv_low, pow_high, pow_low, rhs):
    lane = lax.broadcasted_iota(jnp.int32, (lines, GROUP), 1)
    first = lane == 0
    last = lane == GROUP - 1

    def second_difference(k, part):
        cols = slice(part * GROUP, (part + 1) * GROUP)
        here = src[k + 1, :, cols]
        left = pltpu.roll(jnp.where(last, src[k, :, cols], here), 1, 1)
        right = pltpu.roll(jnp.where(first, src[k + 2, :, cols], here), GROUP - 1, 1)
        return here, left + right - 2.0 * here

    for k in range(GROUPS):
        level = index[step, k]
        coef_re = rhs[0, 0, level]
        coef_im = rhs[0, 1, level]
        base_re, second_re = second_difference(k, 0)
        base_im, second_im = second_difference(k, 1)
        source_re = base_re + coef_re * second_re - coef_im * second_im
        source_im = base_im + coef_re * second_im + coef_im * second_re
        source = jnp.concatenate([source_re, source_im], axis=1)
        dst[k + 1] = product(source, inv_high[level], inv_low[level])

    for at, reach in enumerate((1, 2, 4, 8)):
        count = GROUPS - reach
        moved = dst[1 + reach : 1 + GROUPS].reshape(count * lines, 2 * GROUP)
        added = product(moved, pow_high[at], pow_low[at])
        dst[1 : 1 + count] = dst[1 : 1 + count] + added.reshape(count, lines, 2 * GROUP)


def kernel(
    wave_hbm, inv_hbm, couple_hbm, rhs, recv_index, shot_index,
    out, image,
    wave, inv, couple, inv_high, inv_low, pow_high, pow_low,
    field_a, field_b, unit, column_a, column_b,
    fsend, frecv, bsend, brecv,
    vsend, vrecv, wsend, wrecv, isend, irecv,
    in_sem, fwd_send, fwd_recv, back_send, back_recv, img_send, img_recv,
):
    me = lax.axis_index("plane")
    fr = lax.axis_index("freq")
    cross = me % 8
    along = me // 8

    copies = [
        pltpu.make_async_copy(couple_hbm.at[0], couple, in_sem.at[0]),
        pltpu.make_async_copy(inv_hbm.at[0], inv, in_sem.at[1]),
        pltpu.make_async_copy(wave_hbm.at[0], wave, in_sem.at[2]),
    ]
    for copy in copies:
        copy.start()

    def partner(step):
        return (me + step * 33) % PLANE

    barrier = pltpu.get_barrier_semaphore()

    @pl.loop(1, PLANE)
    def _(step):
        pl.semaphore_signal(barrier, inc=1, device_id=(fr, partner(step)), device_id_type=MESH)

    @pl.loop(1, FREQ)
    def _(step):
        pl.semaphore_signal(barrier, inc=1, device_id=((fr + step) % FREQ, me), device_id_type=MESH)

    passes = dict(inv_high=inv_high, inv_low=inv_low, pow_high=pow_high, pow_low=pow_low, rhs=rhs)

    for ref in (field_a, field_b, unit, column_a, column_b):
        pad = jnp.zeros(ref.shape[1:], F32)
        ref[0] = pad
        ref[GROUPS + 1] = pad

    copies[0].wait()
    power_re = couple[0].T
    power_im = couple[1].T
    for at in range(4):
        store_complex(pow_high, pow_low, at, power_re, power_im)
        if at < 3:
            row = jnp.concatenate([power_re, power_im], axis=1)
            square = product(row, pow_high[at], pow_low[at])
            power_re = square[:, :GROUP]
            power_im = square[:, GROUP:]
    copies[1].wait()

    @pl.loop(0, NV)
    def _(level):
        store_complex(inv_high, inv_low, level, inv[level, 0].T, inv[level, 1].T)

    copies[2].wait()
    for k in range(GROUPS):
        for part in range(2):
            field_a[k + 1, :, part * GROUP : (part + 1) * GROUP] = wave[part, :, k * GROUP : (k + 1) * GROUP]

    line_pass(field_a, field_b, LINES, recv_index, 0, **passes)
    line_pass(field_b, field_a, LINES, recv_index, 1, **passes)

    def exchange(src, dst, h, send, recv):
        @pl.loop(1, PLANE)
        def _(step):
            to = partner(step)
            pltpu.make_async_remote_copy(
                src_ref=src.at[h, to],
                dst_ref=dst.at[h, me],
                send_sem=send.at[h],
                recv_sem=recv.at[h],
                device_id=(fr, to),
                device_id_type=MESH,
            ).start()

        dst[h, me] = src[h, me]

    def all_bytes(ref, h, sem):
        pltpu.make_async_copy(ref.at[h, pl.ds(0, PLANE - 1)], ref.at[h, pl.ds(0, PLANE - 1)], sem.at[h]).wait()

    for h in range(2):
        for big in range(4):
            turned = [
                field_a[1 + 4 * big : 5 + 4 * big, :, part * GROUP : (part + 1) * GROUP]
                .reshape(GROUP, GROUP).T.reshape(4, 4, 8, GROUP)
                for part in range(2)
            ]
            tiles = [turned[part][:, 2 * h + b] for part in range(2) for b in range(2)]
            for y, tile in enumerate(swap_blocks(tiles)):
                first = 4 * (4 * big + y)
                fsend[h, first : first + 4] = tile
        if h == 0:
            pl.semaphore_wait(barrier, PLANE - 1 + FREQ - 1)
        exchange(fsend, frecv, h, fwd_send, fwd_recv)

    spot = lax.broadcasted_iota(jnp.int32, (LINES, GROUP), 1) - lax.broadcasted_iota(
        jnp.int32, (LINES, GROUP), 0
    )
    for k in range(GROUPS):
        unit[k + 1, :, :GROUP] = (spot == LINES * me - k * GROUP).astype(F32)
        unit[k + 1, :, GROUP:] = jnp.zeros((LINES, GROUP), F32)
    line_pass(unit, field_a, LINES, shot_index, 0, **passes)
    for k in range(GROUPS):
        both = field_a[k + 1] * field_b[k + 1]
        terms = both[:, :GROUP] - both[:, GROUP:]
        vsend[k % 2, k // 2 : k // 2 + 1] = jnp.sum(terms, axis=0, keepdims=True)

    @pl.loop(1, 8)
    def _(step):
        to = (cross + step) % 8
        pltpu.make_async_remote_copy(
            src_ref=vsend.at[to // 4],
            dst_ref=vrecv.at[cross],
            send_sem=img_send.at[0],
            recv_sem=img_recv.at[0],
            device_id=(fr, along * 8 + to),
            device_id_type=MESH,
        ).start()

    vrecv[cross] = vsend[cross // 4]

    lane_row = lax.broadcasted_iota(jnp.int32, (1, GROUP), 1)
    mine = lane_row // LINES == me % 4
    diagonal = jnp.zeros((1, GROUP), F32)
    for h in range(2):
        all_bytes(frecv, h, fwd_recv)
        arrived = frecv[h].reshape(GROUPS, 4, 8, GROUP)
        tiles = swap_blocks([arrived[:, q] for q in range(4)])
        for part in range(2):
            for b in range(2):
                column_a[1 : 1 + GROUPS, b * 8 : b * 8 + 8, part * GROUP : (part + 1) * GROUP] = tiles[2 * part + b]
        line_pass(column_a, column_b, HALF, shot_index, 0, **passes)
        line_pass(column_b, column_a, HALF, shot_index, 1, **passes)
        tiles = [
            column_a[1 : 1 + GROUPS, b * 8 : b * 8 + 8, part * GROUP : (part + 1) * GROUP]
            for part in range(2)
            for b in range(2)
        ]
        bsend[h] = jnp.stack(swap_blocks(tiles), axis=1).reshape(PLANE, 8, GROUP)
        exchange(bsend, brecv, h, back_send, back_recv)
        block = column_a[me // 4 + 1, :, :GROUP]
        row = lax.broadcasted_iota(jnp.int32, (HALF, GROUP), 0)
        lane = lax.broadcasted_iota(jnp.int32, (HALF, GROUP), 1)
        kept = jnp.where(lane == (me % 4) * LINES + h * HALF + row, block, 0.0)
        diagonal = diagonal + jnp.sum(kept, axis=0, keepdims=True)
        if h == 0:
            pltpu.make_async_copy(vrecv.at[pl.ds(0, 7)], vrecv.at[pl.ds(0, 7)], img_recv.at[0]).wait()
            sums = jnp.sum(vrecv[...], axis=0)
            for j in range(8):
                wsend[j] = sums[j : j + 1]

            @pl.loop(1, 8)
            def _(step):
                to = (along + step) % 8
                pltpu.make_async_remote_copy(
                    src_ref=wsend.at[to],
                    dst_ref=wrecv.at[along],
                    send_sem=img_send.at[1],
                    recv_sem=img_recv.at[1],
                    device_id=(fr, to * 8 + cross),
                    device_id_type=MESH,
                ).start()

            wrecv[along] = wsend[along]

    pltpu.make_async_copy(wrecv.at[pl.ds(0, 7)], wrecv.at[pl.ds(0, 7)], img_recv.at[1]).wait()
    summed = jnp.where(mine, jnp.sum(wrecv[...], axis=0), 0.0)

    def folded(values):
        values = values + pltpu.roll(values, 64, 1)
        return values + pltpu.roll(values, 32, 1)

    isend[...] = jnp.zeros((8, GROUP), F32)
    isend[0:1] = folded(summed)
    isend[1:2] = folded(diagonal)

    @pl.loop(1, FREQ)
    def _(step):
        pltpu.make_async_remote_copy(
            src_ref=isend,
            dst_ref=irecv.at[fr],
            send_sem=img_send.at[2],
            recv_sem=img_recv.at[2],
            device_id=((fr + step) % FREQ, me),
            device_id_type=MESH,
        ).start()

    irecv[fr] = isend[...]

    for h in range(2):
        all_bytes(brecv, h, back_recv)
    for big in range(4):
        turned = [[None] * 4, [None] * 4]
        for h in range(2):
            tiles = swap_blocks([brecv[h, 4 * (4 * big + y) : 4 * (4 * big + y) + 4] for y in range(4)])
            for part in range(2):
                for b in range(2):
                    turned[part][2 * h + b] = tiles[2 * part + b]
        for part in range(2):
            block = jnp.stack(turned[part], axis=1).reshape(GROUP, GROUP).T
            for y in range(4):
                at = (4 * big + y) * GROUP
                out[0, part, :, at : at + GROUP] = block[y * LINES : (y + 1) * LINES]

    pltpu.make_async_copy(irecv.at[pl.ds(0, 3)], irecv.at[pl.ds(0, 3)], img_recv.at[2]).wait()
    image[...] = (irecv[0] + irecv[1] + irecv[2] + irecv[3])[:2, :LINES]

    for h in range(2):
        all_bytes(fsend, h, fwd_send)
        all_bytes(bsend, h, back_send)
    pltpu.make_async_copy(vrecv.at[pl.ds(0, 7)], vrecv.at[pl.ds(0, 7)], img_send.at[0]).wait()
    pltpu.make_async_copy(wrecv.at[pl.ds(0, 7)], wrecv.at[pl.ds(0, 7)], img_send.at[1]).wait()
    pltpu.make_async_copy(irecv.at[pl.ds(0, 3)], irecv.at[pl.ds(0, 3)], img_send.at[2]).wait()


def shards(wavefield, inv_table, couple_table, rhs_table, recv_index, shot_index):
    hbm = pl.BlockSpec(memory_space=pltpu.HBM)
    vmem = pl.BlockSpec(memory_space=pltpu.VMEM)
    smem = pl.BlockSpec(memory_space=pltpu.SMEM)
    tiles = (2, PLANE, 8, GROUP)
    wide = 2 * GROUP
    return pl.pallas_call(
        kernel,
        out_shape=(
            jax.ShapeDtypeStruct((1, 2, LINES, NX), F32),
            jax.ShapeDtypeStruct((DEPTHS, LINES), F32),
        ),
        in_specs=[hbm, hbm, hbm, smem, smem, smem],
        out_specs=(vmem, vmem),
        scratch_shapes=[
            pltpu.VMEM((2, LINES, NX), F32),
            pltpu.VMEM((NV, 2, GROUP, GROUP), F32),
            pltpu.VMEM((2, GROUP, GROUP), F32),
            pltpu.VMEM((NV, wide, wide), BF16),
            pltpu.VMEM((NV, wide, wide), BF16),
            pltpu.VMEM((4, wide, wide), BF16),
            pltpu.VMEM((4, wide, wide), BF16),
            pltpu.VMEM((GROUPS + 2, LINES, wide), F32),
            pltpu.VMEM((GROUPS + 2, LINES, wide), F32),
            pltpu.VMEM((GROUPS + 2, LINES, wide), F32),
            pltpu.VMEM((GROUPS + 2, HALF, wide), F32),
            pltpu.VMEM((GROUPS + 2, HALF, wide), F32),
            pltpu.VMEM(tiles, F32),
            pltpu.VMEM(tiles, F32),
            pltpu.VMEM(tiles, F32),
            pltpu.VMEM(tiles, F32),
            pltpu.VMEM((2, 8, GROUP), F32),
            pltpu.VMEM((8, 8, GROUP), F32),
            pltpu.VMEM((8, 1, GROUP), F32),
            pltpu.VMEM((8, 1, GROUP), F32),
            pltpu.VMEM((8, GROUP), F32),
            pltpu.VMEM((FREQ, 8, GROUP), F32),
            pltpu.SemaphoreType.DMA((3,)),
            pltpu.SemaphoreType.DMA((2,)),
            pltpu.SemaphoreType.DMA((2,)),
            pltpu.SemaphoreType.DMA((2,)),
            pltpu.SemaphoreType.DMA((2,)),
            pltpu.SemaphoreType.DMA((3,)),
            pltpu.SemaphoreType.DMA((3,)),
        ],
        compiler_params=pltpu.CompilerParams(
            collective_id=0, has_side_effects=True, vmem_limit_bytes=58 << 20
        ),
        cost_estimate=pl.CostEstimate(
            flops=5_000_000_000, bytes_accessed=3_000_000, transcendentals=0
        ),
    )(wavefield, inv_table, couple_table, jnp.swapaxes(rhs_table, 1, 2), recv_index, shot_index)


def solution(mesh):
    placed = (
        P("freq", None, "plane", None),
        P("freq", None, None, None, None),
        P("freq", None, None, None),
        P("freq", None, None),
        P(),
        P(),
    )
    return jax.shard_map(
        shards,
        mesh=mesh,
        in_specs=placed,
        out_specs=(P("freq", None, "plane", None), P(None, "plane")),
        check_vma=False,
    )
```

```python
import functools

import jax
import jax.numpy as jnp
from jax import lax
from jax.experimental import pallas as pl
from jax.experimental.pallas import tpu as pltpu
from jax.sharding import PartitionSpec as P

NX = 2048
GROUP = 128
DEPTHS = 2
NV = 8
GROUPS = NX // GROUP
PLANE = 64
FREQ = 4
LINES = NX // PLANE
HALF = LINES // 2
MESH = pl.DeviceIdType.MESH
F32 = jnp.float32
BF16 = jnp.bfloat16


def split(values):
    high = values.astype(BF16)
    low = (values - high.astype(F32)).astype(BF16)
    return high, low


def dot(left, right):
    return lax.dot_general(left, right, (((1,), (0,)), ((), ())), preferred_element_type=F32)


def product(values, mat_high, mat_low):
    count = values.shape[0]
    high, low = split(values)
    both = dot(jnp.concatenate([high, low], axis=0), mat_high)
    return both[:count] + both[count:] + dot(high, mat_low)


def store_complex(high_ref, low_ref, at, real, imag):
    re_high, re_low = split(real)
    im_high, im_low = split(imag)
    for ref, re_part, im_part in ((high_ref, re_high, im_high), (low_ref, re_low, im_low)):
        ref[at, :GROUP, :GROUP] = re_part
        ref[at, :GROUP, GROUP:] = im_part
        ref[at, GROUP:, :GROUP] = -im_part
        ref[at, GROUP:, GROUP:] = re_part


def swap_blocks(tiles):
    shape = tiles[0].shape
    axis = len(shape) - 1
    lane = lax.broadcasted_iota(jnp.int32, shape, axis)
    lower = lane < 64
    even = (lane // 32) % 2 == 0
    first = [None] * 4
    for a in (0, 1):
        first[a] = jnp.where(lower, tiles[a], pltpu.roll(tiles[a + 2], 64, axis))
        first[a + 2] = jnp.where(lower, pltpu.roll(tiles[a], 64, axis), tiles[a + 2])
    out = [None] * 4
    for a in (0, 2):
        out[a] = jnp.where(even, first[a], pltpu.roll(first[a + 1], 32, axis))
        out[a + 1] = jnp.where(even, pltpu.roll(first[a], 96, axis), first[a + 1])
    return out


def line_pass(src, dst, lines, index, step, inv_high, inv_low, pow_high, pow_low, rhs):
    lane = lax.broadcasted_iota(jnp.int32, (lines, GROUP), 1)
    first = lane == 0
    last = lane == GROUP - 1

    def second_difference(k, part):
        cols = slice(part * GROUP, (part + 1) * GROUP)
        here = src[k + 1, :, cols]
        left = pltpu.roll(jnp.where(last, src[k, :, cols], here), 1, 1)
        right = pltpu.roll(jnp.where(first, src[k + 2, :, cols], here), GROUP - 1, 1)
        return here, left + right - 2.0 * here

    for k in range(GROUPS):
        level = index[step, k]
        coef_re = rhs[0, 0, level]
        coef_im = rhs[0, 1, level]
        base_re, second_re = second_difference(k, 0)
        base_im, second_im = second_difference(k, 1)
        source_re = base_re + coef_re * second_re - coef_im * second_im
        source_im = base_im + coef_re * second_im + coef_im * second_re
        source = jnp.concatenate([source_re, source_im], axis=1)
        dst[k + 1] = product(source, inv_high[level], inv_low[level])

    for at, reach in enumerate((1, 2, 4, 8)):
        count = GROUPS - reach
        moved = dst[1 + reach : 1 + GROUPS].reshape(count * lines, 2 * GROUP)
        added = product(moved, pow_high[at], pow_low[at])
        dst[1 : 1 + count] = dst[1 : 1 + count] + added.reshape(count, lines, 2 * GROUP)


def kernel(
    wave_hbm, inv_hbm, couple_hbm, rhs, recv_index, shot_index,
    out, image,
    wave, inv, couple, inv_high, inv_low, pow_high, pow_low,
    field_a, field_b, unit, column_a, column_b,
    fsend, frecv, bsend, brecv,
    vsend, vrecv, wsend, wrecv, isend, irecv,
    in_sem, fwd_send, fwd_recv, back_send, back_recv, img_send, img_recv,
):
    me = lax.axis_index("plane")
    fr = lax.axis_index("freq")
    cross = me % 8
    along = me // 8

    copies = [
        pltpu.make_async_copy(couple_hbm.at[0], couple, in_sem.at[0]),
        pltpu.make_async_copy(inv_hbm.at[0], inv, in_sem.at[1]),
        pltpu.make_async_copy(wave_hbm.at[0], wave, in_sem.at[2]),
    ]
    for copy in copies:
        copy.start()

    def partner(step):
        return (me + step * 33) % PLANE

    barrier = pltpu.get_barrier_semaphore()

    @pl.loop(1, PLANE)
    def _(step):
        pl.semaphore_signal(barrier, inc=1, device_id=(fr, partner(step)), device_id_type=MESH)

    @pl.loop(1, FREQ)
    def _(step):
        pl.semaphore_signal(barrier, inc=1, device_id=((fr + step) % FREQ, me), device_id_type=MESH)

    passes = dict(inv_high=inv_high, inv_low=inv_low, pow_high=pow_high, pow_low=pow_low, rhs=rhs)

    for ref in (field_a, field_b, unit, column_a, column_b):
        pad = jnp.zeros(ref.shape[1:], F32)
        ref[0] = pad
        ref[GROUPS + 1] = pad

    copies[0].wait()
    power_re = couple[0].T
    power_im = couple[1].T
    for at in range(4):
        store_complex(pow_high, pow_low, at, power_re, power_im)
        if at < 3:
            row = jnp.concatenate([power_re, power_im], axis=1)
            square = product(row, pow_high[at], pow_low[at])
            power_re = square[:, :GROUP]
            power_im = square[:, GROUP:]
    copies[1].wait()

    @pl.loop(0, NV)
    def _(level):
        store_complex(inv_high, inv_low, level, inv[level, 0].T, inv[level, 1].T)

    copies[2].wait()
    for k in range(GROUPS):
        for part in range(2):
            field_a[k + 1, :, part * GROUP : (part + 1) * GROUP] = wave[part, :, k * GROUP : (k + 1) * GROUP]

    line_pass(field_a, field_b, LINES, recv_index, 0, **passes)
    line_pass(field_b, field_a, LINES, recv_index, 1, **passes)

    def exchange(src, dst, h, send, recv):
        @pl.loop(1, PLANE)
        def _(step):
            to = partner(step)
            pltpu.make_async_remote_copy(
                src_ref=src.at[h, to],
                dst_ref=dst.at[h, me],
                send_sem=send.at[h],
                recv_sem=recv.at[h],
                device_id=(fr, to),
                device_id_type=MESH,
            ).start()

        dst[h, me] = src[h, me]

    def all_bytes(ref, h, sem):
        pltpu.make_async_copy(ref.at[h, pl.ds(0, PLANE - 1)], ref.at[h, pl.ds(0, PLANE - 1)], sem.at[h]).wait()

    for h in range(2):
        for big in range(4):
            turned = [
                field_a[1 + 4 * big : 5 + 4 * big, :, part * GROUP : (part + 1) * GROUP]
                .reshape(GROUP, GROUP).T.reshape(4, 4, 8, GROUP)
                for part in range(2)
            ]
            tiles = [turned[part][:, 2 * h + b] for part in range(2) for b in range(2)]
            for y, tile in enumerate(swap_blocks(tiles)):
                first = 4 * (4 * big + y)
                fsend[h, first : first + 4] = tile
        if h == 0:
            pl.semaphore_wait(barrier, PLANE - 1 + FREQ - 1)
        exchange(fsend, frecv, h, fwd_send, fwd_recv)

    spot = lax.broadcasted_iota(jnp.int32, (LINES, GROUP), 1) - lax.broadcasted_iota(
        jnp.int32, (LINES, GROUP), 0
    )
    for k in range(GROUPS):
        unit[k + 1, :, :GROUP] = (spot == LINES * me - k * GROUP).astype(F32)
        unit[k + 1, :, GROUP:] = jnp.zeros((LINES, GROUP), F32)
    line_pass(unit, field_a, LINES, shot_index, 0, **passes)
    for k in range(GROUPS):
        both = field_a[k + 1] * field_b[k + 1]
        terms = both[:, :GROUP] - both[:, GROUP:]
        vsend[k % 2, k // 2 : k // 2 + 1] = jnp.sum(terms, axis=0, keepdims=True)

    @pl.loop(1, 8)
    def _(step):
        to = (cross + step) % 8
        pltpu.make_async_remote_copy(
            src_ref=vsend.at[to // 4],
            dst_ref=vrecv.at[cross],
            send_sem=img_send.at[0],
            recv_sem=img_recv.at[0],
            device_id=(fr, along * 8 + to),
            device_id_type=MESH,
        ).start()

    vrecv[cross] = vsend[cross // 4]

    lane_row = lax.broadcasted_iota(jnp.int32, (1, GROUP), 1)
    mine = lane_row // LINES == me % 4
    diagonal = jnp.zeros((1, GROUP), F32)
    for h in range(2):
        all_bytes(frecv, h, fwd_recv)
        arrived = frecv[h].reshape(GROUPS, 4, 8, GROUP)
        tiles = swap_blocks([arrived[:, q] for q in range(4)])
        for part in range(2):
            for b in range(2):
                column_a[1 : 1 + GROUPS, b * 8 : b * 8 + 8, part * GROUP : (part + 1) * GROUP] = tiles[2 * part + b]
        line_pass(column_a, column_b, HALF, shot_index, 0, **passes)
        line_pass(column_b, column_a, HALF, shot_index, 1, **passes)
        tiles = [
            column_a[1 : 1 + GROUPS, b * 8 : b * 8 + 8, part * GROUP : (part + 1) * GROUP]
            for part in range(2)
            for b in range(2)
        ]
        bsend[h] = jnp.stack(swap_blocks(tiles), axis=1).reshape(PLANE, 8, GROUP)
        exchange(bsend, brecv, h, back_send, back_recv)
        block = column_a[me // 4 + 1, :, :GROUP]
        row = lax.broadcasted_iota(jnp.int32, (HALF, GROUP), 0)
        lane = lax.broadcasted_iota(jnp.int32, (HALF, GROUP), 1)
        kept = jnp.where(lane == (me % 4) * LINES + h * HALF + row, block, 0.0)
        diagonal = diagonal + jnp.sum(kept, axis=0, keepdims=True)
        if h == 0:
            pltpu.make_async_copy(vrecv.at[pl.ds(0, 7)], vrecv.at[pl.ds(0, 7)], img_recv.at[0]).wait()
            sums = jnp.sum(vrecv[...], axis=0)
            for j in range(8):
                wsend[j] = sums[j : j + 1]

            @pl.loop(1, 8)
            def _(step):
                to = (along + step) % 8
                pltpu.make_async_remote_copy(
                    src_ref=wsend.at[to],
                    dst_ref=wrecv.at[along],
                    send_sem=img_send.at[1],
                    recv_sem=img_recv.at[1],
                    device_id=(fr, to * 8 + cross),
                    device_id_type=MESH,
                ).start()

            wrecv[along] = wsend[along]

    pltpu.make_async_copy(wrecv.at[pl.ds(0, 7)], wrecv.at[pl.ds(0, 7)], img_recv.at[1]).wait()
    summed = jnp.where(mine, jnp.sum(wrecv[...], axis=0), 0.0)

    def folded(values):
        values = values + pltpu.roll(values, 64, 1)
        return values + pltpu.roll(values, 32, 1)

    isend[...] = jnp.zeros((8, GROUP), F32)
    isend[0:1] = folded(summed)
    isend[1:2] = folded(diagonal)

    @pl.loop(1, FREQ)
    def _(step):
        pltpu.make_async_remote_copy(
            src_ref=isend,
            dst_ref=irecv.at[fr],
            send_sem=img_send.at[2],
            recv_sem=img_recv.at[2],
            device_id=((fr + step) % FREQ, me),
            device_id_type=MESH,
        ).start()

    irecv[fr] = isend[...]

    def rows_of(h, big):
        return [brecv[h, 4 * (4 * big + y) : 4 * (4 * big + y) + 4] for y in range(4)]

    all_bytes(brecv, 0, back_recv)
    for big in range(4):
        for y, tile in enumerate(swap_blocks(rows_of(0, big))):
            first = 4 * (4 * big + y)
            brecv[0, first : first + 4] = tile
    all_bytes(brecv, 1, back_recv)
    for big in range(4):
        turned = [[None] * 4, [None] * 4]
        for h in range(2):
            tiles = rows_of(h, big)
            if h == 1:
                tiles = swap_blocks(tiles)
            for part in range(2):
                for b in range(2):
                    turned[part][2 * h + b] = tiles[2 * part + b]
        for part in range(2):
            block = jnp.stack(turned[part], axis=1).reshape(GROUP, GROUP).T
            for y in range(4):
                at = (4 * big + y) * GROUP
                out[0, part, :, at : at + GROUP] = block[y * LINES : (y + 1) * LINES]

    pltpu.make_async_copy(irecv.at[pl.ds(0, 3)], irecv.at[pl.ds(0, 3)], img_recv.at[2]).wait()
    image[...] = (irecv[0] + irecv[1] + irecv[2] + irecv[3])[:2, :LINES]

    for h in range(2):
        all_bytes(fsend, h, fwd_send)
        all_bytes(bsend, h, back_send)
    pltpu.make_async_copy(vrecv.at[pl.ds(0, 7)], vrecv.at[pl.ds(0, 7)], img_send.at[0]).wait()
    pltpu.make_async_copy(wrecv.at[pl.ds(0, 7)], wrecv.at[pl.ds(0, 7)], img_send.at[1]).wait()
    pltpu.make_async_copy(irecv.at[pl.ds(0, 3)], irecv.at[pl.ds(0, 3)], img_send.at[2]).wait()


def shards(wavefield, inv_table, couple_table, rhs_table, recv_index, shot_index):
    hbm = pl.BlockSpec(memory_space=pltpu.HBM)
    vmem = pl.BlockSpec(memory_space=pltpu.VMEM)
    smem = pl.BlockSpec(memory_space=pltpu.SMEM)
    tiles = (2, PLANE, 8, GROUP)
    wide = 2 * GROUP
    return pl.pallas_call(
        kernel,
        out_shape=(
            jax.ShapeDtypeStruct((1, 2, LINES, NX), F32),
            jax.ShapeDtypeStruct((DEPTHS, LINES), F32),
        ),
        in_specs=[hbm, hbm, hbm, smem, smem, smem],
        out_specs=(vmem, vmem),
        scratch_shapes=[
            pltpu.VMEM((2, LINES, NX), F32),
            pltpu.VMEM((NV, 2, GROUP, GROUP), F32),
            pltpu.VMEM((2, GROUP, GROUP), F32),
            pltpu.VMEM((NV, wide, wide), BF16),
            pltpu.VMEM((NV, wide, wide), BF16),
            pltpu.VMEM((4, wide, wide), BF16),
            pltpu.VMEM((4, wide, wide), BF16),
            pltpu.VMEM((GROUPS + 2, LINES, wide), F32),
            pltpu.VMEM((GROUPS + 2, LINES, wide), F32),
            pltpu.VMEM((GROUPS + 2, LINES, wide), F32),
            pltpu.VMEM((GROUPS + 2, HALF, wide), F32),
            pltpu.VMEM((GROUPS + 2, HALF, wide), F32),
            pltpu.VMEM(tiles, F32),
            pltpu.VMEM(tiles, F32),
            pltpu.VMEM(tiles, F32),
            pltpu.VMEM(tiles, F32),
            pltpu.VMEM((2, 8, GROUP), F32),
            pltpu.VMEM((8, 8, GROUP), F32),
            pltpu.VMEM((8, 1, GROUP), F32),
            pltpu.VMEM((8, 1, GROUP), F32),
            pltpu.VMEM((8, GROUP), F32),
            pltpu.VMEM((FREQ, 8, GROUP), F32),
            pltpu.SemaphoreType.DMA((3,)),
            pltpu.SemaphoreType.DMA((2,)),
            pltpu.SemaphoreType.DMA((2,)),
            pltpu.SemaphoreType.DMA((2,)),
            pltpu.SemaphoreType.DMA((2,)),
            pltpu.SemaphoreType.DMA((3,)),
            pltpu.SemaphoreType.DMA((3,)),
        ],
        compiler_params=pltpu.CompilerParams(
            collective_id=0, has_side_effects=True, vmem_limit_bytes=58 << 20
        ),
        cost_estimate=pl.CostEstimate(
            flops=5_000_000_000, bytes_accessed=3_000_000, transcendentals=0
        ),
    )(wavefield, inv_table, couple_table, jnp.swapaxes(rhs_table, 1, 2), recv_index, shot_index)


def solution(mesh):
    placed = (
        P("freq", None, "plane", None),
        P("freq", None, None, None, None),
        P("freq", None, None, None),
        P("freq", None, None),
        P(),
        P(),
    )
    return jax.shard_map(
        shards,
        mesh=mesh,
        in_specs=placed,
        out_specs=(P("freq", None, "plane", None), P(None, "plane")),
        check_vma=False,
    )
```
